256 devices in a mesh: kx: 8 (over z_hi, x), ky: 16 (over z_lo, y), af: 2 (over core).
Axes of the slice: x: 4, y: 4, z: 8 (z_hi: 2, z_lo: 4; z = z_hi * 4 + z_lo), core: 2. Of those that a mesh axis runs over, the one named last changes fastest.
Arguments:
- vertex: float32 [2, 8, 16, 768, 768], P(None, 'kx', 'ky', 'af'), may hold values from -1.2 to 1.2
- bare_vertex: float32 [2, 8, 16, 768, 768], P(None, 'kx', 'ky', 'af'), may hold values from -1.2 to 1.2
- bubble_direct: float32 [2, 8, 16, 768], P(None, 'kx', 'ky'), may hold values from 0.1 to 1
- bubble_crossed: float32 [2, 8, 16, 768], P(None, 'kx', 'ky'), may hold values from 0.1 to 1
- shear_in: int32 [2, 768], replicated, may hold values from 0 to 15, as said below
- shear_out: int32 [2, 768], replicated, may hold values from 0 to 15, as said below
Outputs:
- updated: float32 [2, 8, 16, 768, 768], P(None, 'kx', 'ky', 'af')
The draws below stay inside these ranges and needn't reach their ends.
Inputs may be any that keep to these rules, and one draw needn't show every extreme that they name: `shear_in`: row 0 holds each matrix row's shift of the first momentum component (below 16), row 1 that of the second (below 16). Within each half of the 768 rows, every pair (first shift mod 8, second shift) occurs for exactly 3 rows. `shear_out`: same structure as shear_in.
All inputs are finite; a program needn't handle non-finite values.
Results may differ from the reference program's by a relative error of at most 0.000082.
Values sent between devices are 32-bit elements; how exact they have to be, the bound alone decides.
A program may use at most 64 MiB of HBM per device.

```python
import math
import jax
import jax.numpy as jnp
from jax import lax

M = 768
HX = 2
GX = 8
QX = 16
QY = 16


def shear_draw(key, salt):
    base_key = jax.random.fold_in(key, salt)
    lower_key, upper_key, high_key = jax.random.split(base_key, 3)
    half_rows = M // 2
    classes = GX * QY
    combos = jnp.concatenate([jax.random.permutation(lower_key, half_rows), jax.random.permutation(upper_key, half_rows)]) % classes
    high_part = jax.random.randint(high_key, (M,), 0, HX)
    shift_x = combos % GX + GX * high_part
    shift_y = combos // GX
    return jnp.stack([shift_x, shift_y]).astype(jnp.int32)


def draw_shear_in(key, part):
    return shear_draw(key, 11)


def draw_shear_out(key, part):
    return shear_draw(key, 29)


def steps_of(own_key, dims, pieces, least, top_value):
    factor_of = 1.0
    for position, blocks in pieces:
        heights = jax.random.uniform(jax.random.fold_in(jax.random.fold_in(own_key, 6), position), (blocks,), jnp.float32, least / len(pieces), top_value / len(pieces))
        factor_of = factor_of * jnp.repeat(jnp.exp(heights), dims[position] // blocks).reshape((-1,) + (1,) * (len(dims) - 1 - position))
    return factor_of


def bell_draw(rng, dims, spread, bound, cuts=(), kind=jnp.bfloat16):
    drawn = jax.random.normal(rng, dims, jnp.float32) * spread
    if len(cuts) > 0:
        drawn = steps_of(rng, dims, cuts, -0.22, 0.18) * drawn
    return jnp.clip(drawn, min=-bound, max=bound).astype(kind)


def setup_inputs(seed: int = 0) -> dict:
    keys = jax.random.split(jax.random.key(seed), 7)
    vertex = bell_draw(keys[0], (HX, GX, QY, M, M), 0.2, 1.2, ((1, 8), (2, 16), (3, 2)), jnp.float32)
    bare_vertex = bell_draw(keys[1], (HX, GX, QY, M, M), 0.2, 1.2, ((1, 8), (2, 16), (3, 2)), jnp.float32)
    bubble_direct = jnp.clip(jnp.exp(math.log(1.0) - 2.3025851 * jax.random.uniform(keys[2], (HX, GX, QY, M), jnp.float32) ** steps_of(keys[2], (HX, GX, QY, M), ((1, 8), (2, 16)), -0.2, 0.2)), 0.1, 1.0)
    bubble_crossed = jnp.clip(jnp.exp(math.log(1.0) - 2.3025851 * jax.random.uniform(keys[3], (HX, GX, QY, M), jnp.float32) ** steps_of(keys[3], (HX, GX, QY, M), ((1, 8), (2, 16)), -0.2, 0.2)), 0.1, 1.0)
    shear_in = draw_shear_in(jax.random.fold_in(keys[6], 71), 0)
    shear_out = draw_shear_out(jax.random.fold_in(keys[6], 71), 0)
    return dict(vertex=vertex, bare_vertex=bare_vertex, bubble_direct=bubble_direct, bubble_crossed=bubble_crossed, shear_in=shear_in, shear_out=shear_out)


mixing = 0.5


def ladder_all(field, bubble):
    count = QX * QY
    flat_field = field.reshape(count, M, M)
    flat_bubble = bubble.reshape(count, M)

    def single(pair):
        matrix, weights = pair
        return jnp.dot(matrix * weights[None, :], matrix, precision=lax.Precision.HIGHEST, preferred_element_type=jnp.float32)

    return lax.map(single, (flat_field, flat_bubble)).reshape(QX, QY, M, M)


def crossing(field, shear_table):
    source_x = (jnp.arange(QX, dtype=jnp.int32)[:, None] - shear_table[0][None, :]) % QX
    source_y = (jnp.arange(QY, dtype=jnp.int32)[:, None] - shear_table[1][None, :]) % QY
    matrix_rows = jnp.arange(M, dtype=jnp.int32)
    return field[source_x[:, None, :], source_y[None, :, :], matrix_rows[None, None, :]]


def reference(vertex, bare_vertex, bubble_direct, bubble_crossed, shear_in, shear_out):
    field = vertex.reshape(QX, QY, M, M)
    direct_term = ladder_all(field, bubble_direct)
    crossed = crossing(field, shear_in)
    crossed_term = ladder_all(crossed, bubble_crossed)
    returned = crossing(crossed_term, shear_out)
    updated = (1.0 - mixing) * field + mixing * (bare_vertex.reshape(QX, QY, M, M) + direct_term + returned)
    return updated.reshape(HX, GX, QY, M, M)
```

```python
import functools

import jax
import jax.numpy as jnp
from jax import lax
from jax.experimental import pallas as pl
from jax.experimental.pallas import tpu as pltpu
from jax.sharding import PartitionSpec as P

MESH = pl.DeviceIdType.MESH
mixing = 0.5
LANES = 128
NX, NY, NZ = 4, 4, 8
CLASSES_X, CLASSES_Y = 8, 16
CLASSES = CLASSES_X * CLASSES_Y


def halves(value):
    high = value.astype(jnp.bfloat16)
    low = (value - high.astype(jnp.float32)).astype(jnp.bfloat16)
    return high, low


def product(left, right):
    return jnp.dot(left, right, preferred_element_type=jnp.float32)


def column_of(row):
    wide = jnp.broadcast_to(row, (8, row.shape[1])).astype(jnp.float32)
    return wide.T[:, :1].astype(jnp.int32)


def tables(shear, first, rows):
    shift_x = shear[0:1, pl.ds(first, rows)]
    shift_y = shear[1:2, pl.ds(first, rows)]
    group_row = (shift_x & (CLASSES_X - 1)) * CLASSES_Y + shift_y
    group_col = column_of(group_row)
    high_col = column_of(shift_x) // CLASSES_X
    along0 = lax.broadcasted_iota(jnp.int32, (rows, rows), 0)
    along1 = lax.broadcasted_iota(jnp.int32, (rows, rows), 1)
    same = group_row == group_col
    each = rows // CLASSES
    rank_row = jnp.sum(jnp.where(same & (along0 < along1), 1.0, 0.0), axis=0, keepdims=True).astype(jnp.int32)
    rank_col = jnp.sum(jnp.where(same & (along1 < along0), 1.0, 0.0), axis=1, keepdims=True).astype(jnp.int32)
    pack = jnp.where(along0 == group_row * each + rank_row, 1.0, 0.0).astype(jnp.bfloat16)
    unpack = jnp.where(along1 == group_col * each + rank_col, 1.0, 0.0).astype(jnp.bfloat16)
    return group_col // CLASSES_Y, high_col, pack, unpack


def kernel(
    v_hbm, b_hbm, c1, c2, shear_in, shear_out, out_hbm,
    v, vp, acc, pk0, pk1, rv0, rv1, rp0, rp1, ok0, ok1, or0, or1,
    lh, ll, rights, p_in, u_own, u_other, q_mix, u_out, turn_in, turn_out,
    load_sem, store_sem, pair_send, pair_recv, in_send, in_recv, out_send, out_recv,
):
    rows, columns = v.shape[1:]
    strips = columns // LANES
    piece = rows // CLASSES * strips
    lines = rows * strips
    kx, ky, af = lax.axis_index("kx"), lax.axis_index("ky"), lax.axis_index("af")
    x, y, z = kx % NX, ky % NY, (kx // NX) * (NZ // 2) + ky // NY
    own = pl.multiple_of(af * rows, rows)
    other = pl.multiple_of((1 - af) * rows, rows)
    partner = (kx, ky, 1 - af)

    def place(step):
        tx, ty, tz = (x + step // (NY * NZ)) % NX, (y + step // NZ % NY) % NY, (z + step % NZ) % NZ
        return (tz // (NZ // 2)) * NX + tx, (tz % (NZ // 2)) * NY + ty

    loads = [pltpu.make_async_copy(v_hbm, v, load_sem.at[0]), pltpu.make_async_copy(b_hbm, acc, load_sem.at[1])]
    for load in loads:
        load.start()

    barrier = pltpu.get_barrier_semaphore()

    def greet(step, carry):
        tx, ty = place(step)
        pl.semaphore_signal(barrier, inc=1, device_id=(tx, ty, af), device_id_type=MESH)
        return carry

    lax.fori_loop(1, CLASSES, greet, 0)
    pl.semaphore_signal(barrier, inc=1, device_id=partner, device_id_type=MESH)

    class_col, high_col, pack, unpack = tables(shear_in, own, rows)
    p_in[...] = pack
    u_own[...] = unpack
    turn_in[...] = (high_col + (class_col + kx >= CLASSES_X).astype(jnp.int32)) & 1
    loads[0].wait()

    def pack_item(item, into):
        for tile in range(columns // 256):
            span = slice(tile * 256, tile * 256 + 256)
            field = jnp.where(turn_in[...] == 1, v[1 - item, :, span], v[item, :, span])
            high, low = halves(field)
            packed = product(p_in[...], high) + product(p_in[...], low)
            for half in range(2):
                into[pl.ds(2 * tile + half, rows, stride=strips), :] = packed[:, half * LANES : half * LANES + LANES]

    def send_item(source, target, send_sem, recv_sem):
        def send(step, carry):
            tx, ty = place(step)
            group = ((tx + CLASSES_X - kx) % CLASSES_X) * CLASSES_Y + (ty + CLASSES_Y - ky) % CLASSES_Y
            part = pl.ds(group * piece, piece)
            pltpu.make_async_remote_copy(
                src_ref=source.at[part],
                dst_ref=target.at[part],
                send_sem=send_sem,
                recv_sem=recv_sem,
                device_id=(tx, ty, af),
                device_id_type=MESH,
            ).start()
            return carry

        lax.fori_loop(1, CLASSES, send, 0)
        target[0:piece, :] = source[0:piece, :]

    def wait_item(buffer, sem):
        part = buffer.at[pl.ds(piece, lines - piece)]
        pltpu.make_async_copy(part, part, sem).wait()

    def to_partner(source, target, place_of):
        return pltpu.make_async_remote_copy(
            src_ref=source,
            dst_ref=target,
            send_sem=pair_send.at[place_of],
            recv_sem=pair_recv.at[place_of],
            device_id=partner,
            device_id_type=MESH,
        )

    def plain(buffer):
        parts = [halves(buffer[pl.ds(strip, rows, stride=strips), :]) for strip in range(strips)]
        return jnp.concatenate([p[0] for p in parts], axis=1), jnp.concatenate([p[1] for p in parts], axis=1)

    def ladder(tile, rh, rl):
        span = slice(tile * 256, tile * 256 + 256)
        return product(lh[...], rh[:, span]) + product(ll[...], rh[:, span]) + product(lh[...], rl[:, span])

    pack_item(0, pk0)
    pl.semaphore_wait(barrier, CLASSES)

    field_copy = to_partner(v, vp, 0)
    field_copy.start()
    send_item(pk0, rv0, in_send.at[0], in_recv.at[0])
    pack_item(1, pk1)
    send_item(pk1, rv1, in_send.at[1], in_recv.at[1])

    u_other[...] = tables(shear_in, other, rows)[3]
    class_col, high_col, pack, unpack = tables(shear_out, own, rows)
    turn_out[...] = (high_col + (class_col > kx).astype(jnp.int32)) & 1
    u_out[...] = unpack
    q_mix[...] = product(pack, u_own[...]).astype(jnp.bfloat16)

    loads[1].wait()
    field_copy.wait()
    for item in range(2):
        rh, rl = rights.at[0, item], rights.at[1, item]
        rh[pl.ds(own, rows), :], rl[pl.ds(own, rows), :] = halves(v[item])
        rh[pl.ds(other, rows), :], rl[pl.ds(other, rows), :] = halves(vp[item])
        lh[...], ll[...] = halves(v[item] * c1[item : item + 1, :])
        for tile in range(columns // 256):
            span = slice(tile * 256, tile * 256 + 256)
            acc[item, :, span] = (1.0 - mixing) * v[item, :, span] + mixing * (acc[item, :, span] + ladder(tile, rh, rl))

    def crossed_item(item, arrived, arrived_pair, into):
        rh, rl = rights.at[0, 2 + item], rights.at[1, 2 + item]
        wait_item(arrived, in_recv.at[item])
        copy = to_partner(arrived, arrived_pair, 1 + item)
        copy.start()
        high, low = plain(arrived)
        rh[pl.ds(own, rows), :] = product(u_own[...], high).astype(jnp.bfloat16)
        rl[pl.ds(own, rows), :] = product(u_own[...], low).astype(jnp.bfloat16)
        left = product(q_mix[...], high) + product(q_mix[...], low)
        lh[...], ll[...] = halves(left * c2[item : item + 1, :])
        copy.wait()
        high, low = plain(arrived_pair)
        rh[pl.ds(other, rows), :] = product(u_other[...], high).astype(jnp.bfloat16)
        rl[pl.ds(other, rows), :] = product(u_other[...], low).astype(jnp.bfloat16)
        for tile in range(columns // 256):
            term = ladder(tile, rh, rl)
            for half in range(2):
                into[pl.ds(2 * tile + half, rows, stride=strips), :] = term[:, half * LANES : half * LANES + LANES]

    crossed_item(0, rv0, rp0, ok0)
    send_item(ok0, or0, out_send.at[0], out_recv.at[0])
    crossed_item(1, rv1, rp1, ok1)
    send_item(ok1, or1, out_send.at[1], out_recv.at[1])

    def returned_item(item, arrived):
        wait_item(arrived, out_recv.at[item])
        high, low = plain(arrived)
        term = mixing * (product(u_out[...], high) + product(u_out[...], low))
        turned = turn_out[...] == 1
        acc[item] += jnp.where(turned, 0.0, term)
        acc[1 - item] += jnp.where(turned, term, 0.0)

    returned_item(0, or0)
    returned_item(1, or1)
    store = pltpu.make_async_copy(acc, out_hbm, store_sem)
    store.start()
    for item, (first, second) in enumerate(((pk0, ok0), (pk1, ok1))):
        wait_item(first, in_send.at[item])
        wait_item(second, out_send.at[item])
    store.wait()


def body(vertex, bare_vertex, bubble_direct, bubble_crossed, shear_in, shear_out):
    items, _, _, rows, columns = vertex.shape
    shape = (items, rows, columns)
    lines = (rows * columns // LANES, LANES)
    vmem = pl.BlockSpec(memory_space=pltpu.VMEM)
    anywhere = pl.BlockSpec(memory_space=pl.ANY)
    wide, real = jnp.float32, jnp.bfloat16
    dma = pltpu.SemaphoreType.DMA
    updated = pl.pallas_call(
        kernel,
        out_shape=jax.ShapeDtypeStruct(shape, wide),
        in_specs=[anywhere, anywhere, vmem, vmem, vmem, vmem],
        out_specs=anywhere,
        scratch_shapes=[pltpu.VMEM(shape, wide)] * 3
        + [pltpu.VMEM(lines, wide)] * 10
        + [pltpu.VMEM((rows, columns), real)] * 2
        + [pltpu.VMEM((2, 4, columns, columns), real)]
        + [pltpu.VMEM((rows, rows), real)] * 5
        + [pltpu.VMEM((rows, 1), jnp.int32)] * 2
        + [dma((2,)), dma, dma((3,)), dma((3,)), dma((2,)), dma((2,)), dma((2,)), dma((2,))],
        compiler_params=pltpu.CompilerParams(
            collective_id=0, has_side_effects=True, vmem_limit_bytes=56 * 2**20
        ),
    )(
        vertex.reshape(shape),
        bare_vertex.reshape(shape),
        bubble_direct.reshape(items, columns),
        bubble_crossed.reshape(items, columns),
        shear_in,
        shear_out,
    )
    return updated.reshape(vertex.shape)


def solution(mesh):
    placed = (
        P(None, "kx", "ky", "af", None),
        P(None, "kx", "ky", "af", None),
        P(None, "kx", "ky", None),
        P(None, "kx", "ky", None),
        P(),
        P(),
    )
    return jax.shard_map(
        body, mesh=mesh, in_specs=placed, out_specs=P(None, "kx", "ky", "af", None), check_vma=False
    )
```

```python
import functools

import jax
import jax.numpy as jnp
from jax import lax
from jax.experimental import pallas as pl
from jax.experimental.pallas import tpu as pltpu
from jax.sharding import PartitionSpec as P

MESH = pl.DeviceIdType.MESH
mixing = 0.5
LANES = 128
NX, NY, NZ = 4, 4, 8
CLASSES_X, CLASSES_Y = 8, 16
CLASSES = CLASSES_X * CLASSES_Y


def halves(value):
    high = value.astype(jnp.bfloat16)
    low = (value - high.astype(jnp.float32)).astype(jnp.bfloat16)
    return high, low


def product(left, right):
    return jnp.dot(left, right, preferred_element_type=jnp.float32)


def column_of(row):
    wide = jnp.broadcast_to(row, (8, row.shape[1])).astype(jnp.float32)
    return wide.T[:, :1].astype(jnp.int32)


def tables(shear, first, rows):
    shift_x = shear[0:1, pl.ds(first, rows)]
    shift_y = shear[1:2, pl.ds(first, rows)]
    group_row = (shift_x & (CLASSES_X - 1)) * CLASSES_Y + shift_y
    group_col = column_of(group_row)
    high_col = column_of(shift_x) // CLASSES_X
    along0 = lax.broadcasted_iota(jnp.int32, (rows, rows), 0)
    along1 = lax.broadcasted_iota(jnp.int32, (rows, rows), 1)
    same = group_row == group_col
    each = rows // CLASSES
    rank_row = jnp.sum(jnp.where(same & (along0 < along1), 1.0, 0.0), axis=0, keepdims=True).astype(jnp.int32)
    rank_col = jnp.sum(jnp.where(same & (along1 < along0), 1.0, 0.0), axis=1, keepdims=True).astype(jnp.int32)
    pack = jnp.where(along0 == group_row * each + rank_row, 1.0, 0.0).astype(jnp.bfloat16)
    unpack = jnp.where(along1 == group_col * each + rank_col, 1.0, 0.0).astype(jnp.bfloat16)
    return group_col // CLASSES_Y, high_col, pack, unpack


def kernel(
    v_hbm, b_hbm, c1, c2, shear_in, shear_out, acc_hbm, or1, u_out, turn_out,
    v, vp, acc, pk0, pk1, rv0, rv1, rp0, rp1, ok0, ok1, or0,
    lh, ll, rights, p_in, u_own, u_other, q_mix, turn_in,
    load_sem, store_sem, pair_send, pair_recv, in_send, in_recv, out_send, out_recv,
):
    rows, columns = v.shape[1:]
    strips = columns // LANES
    piece = rows // CLASSES * strips
    lines = rows * strips
    kx, ky, af = lax.axis_index("kx"), lax.axis_index("ky"), lax.axis_index("af")
    x, y, z = kx & 3, ky & 3, (kx >> 2) * 4 + (ky >> 2)
    own = pl.multiple_of(af * rows, rows)
    other = pl.multiple_of((1 - af) * rows, rows)
    partner = (kx, ky, 1 - af)

    def place(step):
        tx, ty, tz = (x + (step >> 5)) & 3, (y + (step >> 3)) & 3, (z + step) & 7
        return (tz >> 2) * NX + tx, (tz & 3) * NY + ty

    loads = [pltpu.make_async_copy(v_hbm, v, load_sem.at[0]), pltpu.make_async_copy(b_hbm, acc, load_sem.at[1])]
    for load in loads:
        load.start()

    barrier = pltpu.get_barrier_semaphore()

    def greet(step, carry):
        tx, ty = place(step)
        pl.semaphore_signal(barrier, inc=1, device_id=(tx, ty, af), device_id_type=MESH)
        return carry

    lax.fori_loop(1, CLASSES, greet, 0)
    pl.semaphore_signal(barrier, inc=1, device_id=partner, device_id_type=MESH)

    class_col, high_col, pack, unpack = tables(shear_in, own, rows)
    p_in[...] = pack
    u_own[...] = unpack
    turn_in[...] = (high_col + (class_col + kx >= CLASSES_X).astype(jnp.int32)) & 1
    loads[0].wait()

    def pack_item(item, into):
        for tile in range(columns // 256):
            span = slice(tile * 256, tile * 256 + 256)
            field = jnp.where(turn_in[...] == 1, v[1 - item, :, span], v[item, :, span])
            high, low = halves(field)
            packed = product(p_in[...], high) + product(p_in[...], low)
            for half in range(2):
                into[pl.ds(2 * tile + half, rows, stride=strips), :] = packed[:, half * LANES : half * LANES + LANES]

    def send_item(source, target, send_sem, recv_sem):
        def send(step, carry):
            tx, ty = place(step)
            group = ((tx - kx) & (CLASSES_X - 1)) * CLASSES_Y + ((ty - ky) & (CLASSES_Y - 1))
            part = pl.ds(group * piece, piece)
            pltpu.make_async_remote_copy(
                src_ref=source.at[part],
                dst_ref=target.at[part],
                send_sem=send_sem,
                recv_sem=recv_sem,
                device_id=(tx, ty, af),
                device_id_type=MESH,
            ).start()
            return carry

        lax.fori_loop(1, CLASSES, send, 0)

    def wait_item(buffer, sem):
        part = buffer.at[pl.ds(piece, lines - piece)]
        pltpu.make_async_copy(part, part, sem).wait()

    def to_partner(source, target, place_of):
        return pltpu.make_async_remote_copy(
            src_ref=source,
            dst_ref=target,
            send_sem=pair_send.at[place_of],
            recv_sem=pair_recv.at[place_of],
            device_id=partner,
            device_id_type=MESH,
        )

    def plain(buffer):
        parts = [halves(buffer[pl.ds(strip, rows, stride=strips), :]) for strip in range(strips)]
        return jnp.concatenate([p[0] for p in parts], axis=1), jnp.concatenate([p[1] for p in parts], axis=1)

    def ladder(tile, rh, rl):
        span = slice(tile * 256, tile * 256 + 256)
        return product(lh[...], rh[:, span]) + product(ll[...], rh[:, span]) + product(lh[...], rl[:, span])

    pack_item(0, pk0)
    pl.semaphore_wait(barrier, CLASSES)

    field_copy = to_partner(v, vp, 0)
    field_copy.start()
    send_item(pk0, rv0, in_send.at[0], in_recv.at[0])
    rv0[0:piece, :] = pk0[0:piece, :]
    pack_item(1, pk1)
    send_item(pk1, rv1, in_send.at[1], in_recv.at[1])
    rv1[0:piece, :] = pk1[0:piece, :]

    u_other[...] = tables(shear_in, other, rows)[3]
    class_col, high_col, pack, unpack = tables(shear_out, own, rows)
    turn_out[...] = (high_col + (class_col > kx).astype(jnp.int32)) & 1
    u_out[...] = unpack
    q_mix[...] = product(pack, u_own[...]).astype(jnp.bfloat16)

    loads[1].wait()
    field_copy.wait()
    for item in range(2):
        rh, rl = rights.at[0, item], rights.at[1, item]
        rh[pl.ds(own, rows), :], rl[pl.ds(own, rows), :] = halves(v[item])
        rh[pl.ds(other, rows), :], rl[pl.ds(other, rows), :] = halves(vp[item])
        lh[...], ll[...] = halves(v[item] * c1[item, 0])
        for tile in range(columns // 256):
            span = slice(tile * 256, tile * 256 + 256)
            acc[item, :, span] = (1.0 - mixing) * v[item, :, span] + mixing * (acc[item, :, span] + ladder(tile, rh, rl))

    def crossed_item(item, arrived, arrived_pair, into):
        rh, rl = rights.at[0, 2 + item], rights.at[1, 2 + item]
        wait_item(arrived, in_recv.at[item])
        copy = to_partner(arrived, arrived_pair, 1 + item)
        copy.start()
        high, low = plain(arrived)
        rh[pl.ds(own, rows), :] = product(u_own[...], high).astype(jnp.bfloat16)
        rl[pl.ds(own, rows), :] = product(u_own[...], low).astype(jnp.bfloat16)
        left = product(q_mix[...], high) + product(q_mix[...], low)
        lh[...], ll[...] = halves(left * c2[item, 0])
        copy.wait()
        high, low = plain(arrived_pair)
        rh[pl.ds(other, rows), :] = product(u_other[...], high).astype(jnp.bfloat16)
        rl[pl.ds(other, rows), :] = product(u_other[...], low).astype(jnp.bfloat16)
        for tile in range(columns // 256):
            term = ladder(tile, rh, rl)
            for half in range(2):
                into[pl.ds(2 * tile + half, rows, stride=strips), :] = term[:, half * LANES : half * LANES + LANES]

    crossed_item(0, rv0, rp0, ok0)
    send_item(ok0, or0, out_send.at[0], out_recv.at[0])
    or0[0:piece, :] = ok0[0:piece, :]
    crossed_item(1, rv1, rp1, ok1)
    send_item(ok1, or1, out_send.at[1], out_recv.at[1])
    kept = pltpu.make_async_copy(ok1.at[pl.ds(0, piece)], or1.at[pl.ds(0, piece)], store_sem.at[1])
    kept.start()

    wait_item(or0, out_recv.at[0])
    high, low = plain(or0)
    term = mixing * (product(u_out[...], high) + product(u_out[...], low))
    turned = turn_out[...] == 1
    acc[0] += jnp.where(turned, 0.0, term)
    acc[1] += jnp.where(turned, term, 0.0)
    store = pltpu.make_async_copy(acc, acc_hbm, store_sem.at[0])
    store.start()
    for item, (first, second) in enumerate(((pk0, ok0), (pk1, ok1))):
        wait_item(first, in_send.at[item])
        wait_item(second, out_send.at[item])
    store.wait()
    kept.wait()
    wait_item(or1, out_recv.at[1])


def finish(acc, arrived, u_out, turn_out, out):
    rows, wide = out.shape[1:]
    strips = arrived.shape[0] // rows
    parts = [
        halves(arrived[pl.ds(pl.program_id(0) * (wide // LANES) + strip, rows, stride=strips), :])
        for strip in range(wide // LANES)
    ]
    high, low = jnp.concatenate([p[0] for p in parts], axis=1), jnp.concatenate([p[1] for p in parts], axis=1)
    term = mixing * (product(u_out[...], high) + product(u_out[...], low))
    turned = turn_out[...] == 1
    out[0] = acc[0] + jnp.where(turned, term, 0.0)
    out[1] = acc[1] + jnp.where(turned, 0.0, term)


def body(vertex, bare_vertex, bubble_direct, bubble_crossed, shear_in, shear_out):
    items, _, _, rows, columns = vertex.shape
    shape = (items, rows, columns)
    lines = (rows * columns // LANES, LANES)
    vmem = pl.BlockSpec(memory_space=pltpu.VMEM)
    anywhere = pl.BlockSpec(memory_space=pl.ANY)
    wide, real = jnp.float32, jnp.bfloat16
    dma = pltpu.SemaphoreType.DMA
    partial, arrived, order, turn = pl.pallas_call(
        kernel,
        out_shape=[
            jax.ShapeDtypeStruct(shape, wide),
            jax.ShapeDtypeStruct(lines, wide),
            jax.ShapeDtypeStruct((rows, rows), real),
            jax.ShapeDtypeStruct((rows, 1), jnp.int32),
        ],
        in_specs=[anywhere, anywhere, vmem, vmem, vmem, vmem],
        out_specs=[anywhere, anywhere, vmem, vmem],
        scratch_shapes=[pltpu.VMEM(shape, wide)] * 3
        + [pltpu.VMEM(lines, wide)] * 9
        + [pltpu.VMEM((rows, columns), real)] * 2
        + [pltpu.VMEM((2, 4, columns, columns), real)]
        + [pltpu.VMEM((rows, rows), real)] * 4
        + [pltpu.VMEM((rows, 1), jnp.int32)]
        + [dma((2,)), dma((2,)), dma((3,)), dma((3,)), dma((2,)), dma((2,)), dma((2,)), dma((2,))],
        compiler_params=pltpu.CompilerParams(
            collective_id=0, has_side_effects=True, vmem_limit_bytes=56 * 2**20
        ),
    )(
        vertex.reshape(shape),
        bare_vertex.reshape(shape),
        bubble_direct,
        bubble_crossed,
        shear_in,
        shear_out,
    )
    step = 2 * LANES
    strip = pl.BlockSpec((items, rows, step), lambda i: (0, 0, i))
    updated = pl.pallas_call(
        finish,
        grid=(columns // step,),
        out_shape=jax.ShapeDtypeStruct(shape, wide),
        in_specs=[
            strip,
            pl.BlockSpec(lines, lambda i: (0, 0)),
            pl.BlockSpec((rows, rows), lambda i: (0, 0)),
            pl.BlockSpec((rows, 1), lambda i: (0, 0)),
        ],
        out_specs=strip,
        compiler_params=pltpu.CompilerParams(vmem_limit_bytes=60 * 2**20),
    )(partial, arrived, order, turn)
    return updated.reshape(vertex.shape)


def solution(mesh):
    placed = (
        P(None, "kx", "ky", "af", None),
        P(None, "kx", "ky", "af", None),
        P(None, "kx", "ky", None),
        P(None, "kx", "ky", None),
        P(),
        P(),
    )
    return jax.shard_map(
        body, mesh=mesh, in_specs=placed, out_specs=P(None, "kx", "ky", "af", None), check_vma=False
    )
```

```python
import functools

import jax
import jax.numpy as jnp
from jax import lax
from jax.experimental import pallas as pl
from jax.experimental.pallas import tpu as pltpu
from jax.sharding import PartitionSpec as P

MESH = pl.DeviceIdType.MESH
mixing = 0.5
LANES = 128
NX, NY, NZ = 4, 4, 8
CLASSES_X, CLASSES_Y = 8, 16
CLASSES = CLASSES_X * CLASSES_Y


def halves(value):
    high = value.astype(jnp.bfloat16)
    low = (value - high.astype(jnp.float32)).astype(jnp.bfloat16)
    return high, low


def product(left, right):
    return jnp.dot(left, right, preferred_element_type=jnp.float32)


def column_of(row):
    wide = jnp.broadcast_to(row, (8, row.shape[1])).astype(jnp.float32)
    return wide.T[:, :1].astype(jnp.int32)


def tables(shear, first, rows):
    shift_x = shear[0:1, pl.ds(first, rows)]
    shift_y = shear[1:2, pl.ds(first, rows)]
    group_row = (shift_x & (CLASSES_X - 1)) * CLASSES_Y + shift_y
    group_col = column_of(group_row)
    high_col = column_of(shift_x) // CLASSES_X
    along0 = lax.broadcasted_iota(jnp.int32, (rows, rows), 0)
    along1 = lax.broadcasted_iota(jnp.int32, (rows, rows), 1)
    same = group_row == group_col
    each = rows // CLASSES
    rank_row = jnp.sum(jnp.where(same & (along0 < along1), 1.0, 0.0), axis=0, keepdims=True).astype(jnp.int32)
    rank_col = jnp.sum(jnp.where(same & (along1 < along0), 1.0, 0.0), axis=1, keepdims=True).astype(jnp.int32)
    pack = jnp.where(along0 == group_row * each + rank_row, 1.0, 0.0).astype(jnp.bfloat16)
    unpack = jnp.where(along1 == group_col * each + rank_col, 1.0, 0.0).astype(jnp.bfloat16)
    return group_col // CLASSES_Y, high_col, pack, unpack


def kernel(
    v_hbm, b_hbm, c1, c2, shear_in, shear_out, acc, or1, u_out, turn_out,
    v, vp, pk0, pk1, rv0, rv1, rp0, rp1, ok0, ok1, or0,
    lh, ll, rights, p_in, u_own, u_other, q_mix, turn_in,
    load_sem, pair_send, pair_recv, in_send, in_recv, out_send, out_recv,
):
    rows, columns = v.shape[1:]
    strips = columns // LANES
    piece = rows // CLASSES * strips
    lines = rows * strips
    kx, ky, af = lax.axis_index("kx"), lax.axis_index("ky"), lax.axis_index("af")
    x, y, z = kx & 3, ky & 3, (kx >> 2) * 4 + (ky >> 2)
    own = pl.multiple_of(af * rows, rows)
    other = pl.multiple_of((1 - af) * rows, rows)
    partner = (kx, ky, 1 - af)

    def place(step):
        tx, ty, tz = (x + (step >> 5)) & 3, (y + (step >> 3)) & 3, (z + step) & 7
        return (tz >> 2) * NX + tx, (tz & 3) * NY + ty

    loads = [pltpu.make_async_copy(v_hbm, v, load_sem.at[0]), pltpu.make_async_copy(b_hbm, acc, load_sem.at[1])]
    for load in loads:
        load.start()

    barrier = pltpu.get_barrier_semaphore()

    def greet(step, carry):
        tx, ty = place(step)
        pl.semaphore_signal(barrier, inc=1, device_id=(tx, ty, af), device_id_type=MESH)
        return carry

    lax.fori_loop(1, CLASSES, greet, 0)
    pl.semaphore_signal(barrier, inc=1, device_id=partner, device_id_type=MESH)

    class_col, high_col, pack, unpack = tables(shear_in, own, rows)
    p_in[...] = pack
    u_own[...] = unpack
    turn_in[...] = (high_col + (class_col + kx >= CLASSES_X).astype(jnp.int32)) & 1
    loads[0].wait()

    def pack_item(item, into):
        for tile in range(columns // 256):
            span = slice(tile * 256, tile * 256 + 256)
            field = jnp.where(turn_in[...] == 1, v[1 - item, :, span], v[item, :, span])
            high, low = halves(field)
            packed = product(p_in[...], high) + product(p_in[...], low)
            for half in range(2):
                into[pl.ds(2 * tile + half, rows, stride=strips), :] = packed[:, half * LANES : half * LANES + LANES]

    def send_item(source, target, send_sem, recv_sem):
        def send(step, carry):
            tx, ty = place(step)
            group = ((tx - kx) & (CLASSES_X - 1)) * CLASSES_Y + ((ty - ky) & (CLASSES_Y - 1))
            part = pl.ds(group * piece, piece)
            pltpu.make_async_remote_copy(
                src_ref=source.at[part],
                dst_ref=target.at[part],
                send_sem=send_sem,
                recv_sem=recv_sem,
                device_id=(tx, ty, af),
                device_id_type=MESH,
            ).start()
            return carry

        lax.fori_loop(1, CLASSES, send, 0)

    def wait_item(buffer, sem):
        part = buffer.at[pl.ds(piece, lines - piece)]
        pltpu.make_async_copy(part, part, sem).wait()

    def to_partner(source, target, place_of):
        return pltpu.make_async_remote_copy(
            src_ref=source,
            dst_ref=target,
            send_sem=pair_send.at[place_of],
            recv_sem=pair_recv.at[place_of],
            device_id=partner,
            device_id_type=MESH,
        )

    def plain(buffer):
        parts = [halves(buffer[pl.ds(strip, rows, stride=strips), :]) for strip in range(strips)]
        return jnp.concatenate([p[0] for p in parts], axis=1), jnp.concatenate([p[1] for p in parts], axis=1)

    def ladder(tile, rh, rl):
        span = slice(tile * 256, tile * 256 + 256)
        return product(lh[...], rh[:, span]) + product(ll[...], rh[:, span]) + product(lh[...], rl[:, span])

    pack_item(0, pk0)
    pl.semaphore_wait(barrier, CLASSES)

    field_copy = to_partner(v, vp, 0)
    field_copy.start()
    send_item(pk0, rv0, in_send.at[0], in_recv.at[0])
    rv0[0:piece, :] = pk0[0:piece, :]
    pack_item(1, pk1)
    send_item(pk1, rv1, in_send.at[1], in_recv.at[1])
    rv1[0:piece, :] = pk1[0:piece, :]

    u_other[...] = tables(shear_in, other, rows)[3]
    class_col, high_col, pack, unpack = tables(shear_out, own, rows)
    turn_out[...] = (high_col + (class_col > kx).astype(jnp.int32)) & 1
    u_out[...] = unpack
    q_mix[...] = product(pack, u_own[...]).astype(jnp.bfloat16)

    loads[1].wait()
    field_copy.wait()
    for item in range(2):
        rh, rl = rights.at[0, item], rights.at[1, item]
        rh[pl.ds(own, rows), :], rl[pl.ds(own, rows), :] = halves(v[item])
        rh[pl.ds(other, rows), :], rl[pl.ds(other, rows), :] = halves(vp[item])
        lh[...], ll[...] = halves(v[item] * c1[item, 0])
        for tile in range(columns // 256):
            span = slice(tile * 256, tile * 256 + 256)
            acc[item, :, span] = (1.0 - mixing) * v[item, :, span] + mixing * (acc[item, :, span] + ladder(tile, rh, rl))

    def crossed_item(item, arrived, arrived_pair, into):
        rh, rl = rights.at[0, 2 + item], rights.at[1, 2 + item]
        wait_item(arrived, in_recv.at[item])
        copy = to_partner(arrived, arrived_pair, 1 + item)
        copy.start()
        high, low = plain(arrived)
        rh[pl.ds(own, rows), :] = product(u_own[...], high).astype(jnp.bfloat16)
        rl[pl.ds(own, rows), :] = product(u_own[...], low).astype(jnp.bfloat16)
        left = product(q_mix[...], high) + product(q_mix[...], low)
        lh[...], ll[...] = halves(left * c2[item, 0])
        copy.wait()
        high, low = plain(arrived_pair)
        rh[pl.ds(other, rows), :] = product(u_other[...], high).astype(jnp.bfloat16)
        rl[pl.ds(other, rows), :] = product(u_other[...], low).astype(jnp.bfloat16)
        for tile in range(columns // 256):
            term = ladder(tile, rh, rl)
            for half in range(2):
                into[pl.ds(2 * tile + half, rows, stride=strips), :] = term[:, half * LANES : half * LANES + LANES]

    crossed_item(0, rv0, rp0, ok0)
    send_item(ok0, or0, out_send.at[0], out_recv.at[0])
    or0[0:piece, :] = ok0[0:piece, :]
    crossed_item(1, rv1, rp1, ok1)
    send_item(ok1, or1, out_send.at[1], out_recv.at[1])
    or1[0:piece, :] = ok1[0:piece, :]

    wait_item(or0, out_recv.at[0])
    high, low = plain(or0)
    term = mixing * (product(u_out[...], high) + product(u_out[...], low))
    turned = turn_out[...] == 1
    acc[0] += jnp.where(turned, 0.0, term)
    acc[1] += jnp.where(turned, term, 0.0)
    for item, (first, second) in enumerate(((pk0, ok0), (pk1, ok1))):
        wait_item(first, in_send.at[item])
        wait_item(second, out_send.at[item])
    wait_item(or1, out_recv.at[1])


def finish(acc, arrived, u_out, turn_out, out_hbm, out, store_sem):
    items, rows, columns = out.shape
    strips = columns // LANES
    turned = turn_out[...] == 1
    stores = []
    for tile in range(columns // 256):
        span = slice(tile * 256, tile * 256 + 256)
        parts = [halves(arrived[pl.ds(2 * tile + half, rows, stride=strips), :]) for half in range(2)]
        high, low = jnp.concatenate([p[0] for p in parts], axis=1), jnp.concatenate([p[1] for p in parts], axis=1)
        term = mixing * (product(u_out[...], high) + product(u_out[...], low))
        out[0, :, span] = acc[0, :, span] + jnp.where(turned, term, 0.0)
        out[1, :, span] = acc[1, :, span] + jnp.where(turned, 0.0, term)
        stores.append(pltpu.make_async_copy(out.at[:, :, span], out_hbm.at[:, :, span], store_sem.at[tile]))
        stores[-1].start()
    for store in stores:
        store.wait()


def body(vertex, bare_vertex, bubble_direct, bubble_crossed, shear_in, shear_out):
    items, _, _, rows, columns = vertex.shape
    shape = (items, rows, columns)
    lines = (rows * columns // LANES, LANES)
    vmem = pl.BlockSpec(memory_space=pltpu.VMEM)
    anywhere = pl.BlockSpec(memory_space=pl.ANY)
    wide, real = jnp.float32, jnp.bfloat16
    dma = pltpu.SemaphoreType.DMA
    partial, arrived, order, turn = pl.pallas_call(
        kernel,
        out_shape=[
            pltpu.VMEM(shape, wide),
            pltpu.VMEM(lines, wide),
            pltpu.VMEM((rows, rows), real),
            pltpu.VMEM((rows, 1), jnp.int32),
        ],
        in_specs=[anywhere, anywhere, vmem, vmem, vmem, vmem],
        out_specs=[vmem] * 4,
        scratch_shapes=[pltpu.VMEM(shape, wide)] * 2
        + [pltpu.VMEM(lines, wide)] * 9
        + [pltpu.VMEM((rows, columns), real)] * 2
        + [pltpu.VMEM((2, 4, columns, columns), real)]
        + [pltpu.VMEM((rows, rows), real)] * 4
        + [pltpu.VMEM((rows, 1), jnp.int32)]
        + [dma((2,)), dma((3,)), dma((3,)), dma((2,)), dma((2,)), dma((2,)), dma((2,))],
        compiler_params=pltpu.CompilerParams(
            collective_id=0, has_side_effects=True, vmem_limit_bytes=60 * 2**20
        ),
    )(
        vertex.reshape(shape),
        bare_vertex.reshape(shape),
        bubble_direct,
        bubble_crossed,
        shear_in,
        shear_out,
    )
    updated = pl.pallas_call(
        finish,
        out_shape=jax.ShapeDtypeStruct(shape, wide),
        in_specs=[vmem] * 4,
        out_specs=anywhere,
        scratch_shapes=[pltpu.VMEM(shape, wide), dma((columns // 256,))],
        compiler_params=pltpu.CompilerParams(vmem_limit_bytes=16 * 2**20),
    )(partial, arrived, order, turn)
    return updated.reshape(vertex.shape)


def solution(mesh):
    placed = (
        P(None, "kx", "ky", "af", None),
        P(None, "kx", "ky", "af", None),
        P(None, "kx", "ky", None),
        P(None, "kx", "ky", None),
        P(),
        P(),
    )
    return jax.shard_map(
        body, mesh=mesh, in_specs=placed, out_specs=P(None, "kx", "ky", "af", None), check_vma=False
    )
```

```python
import functools

import jax
import jax.numpy as jnp
from jax import lax
from jax.experimental import pallas as pl
from jax.experimental.pallas import tpu as pltpu
from jax.sharding import PartitionSpec as P

MESH = pl.DeviceIdType.MESH
mixing = 0.5
LANES = 128
NX, NY, NZ = 4, 4, 8
CLASSES_X, CLASSES_Y = 8, 16
CLASSES = CLASSES_X * CLASSES_Y


def halves(value):
    high = value.astype(jnp.bfloat16)
    low = (value - high.astype(jnp.float32)).astype(jnp.bfloat16)
    return high, low


def product(left, right):
    return jnp.dot(left, right, preferred_element_type=jnp.float32)


def column_of(row):
    wide = jnp.broadcast_to(row, (8, row.shape[1])).astype(jnp.float32)
    return wide.T[:, :1].astype(jnp.int32)


def tables(shear, first, rows):
    shift_x = shear[0:1, pl.ds(first, rows)]
    shift_y = shear[1:2, pl.ds(first, rows)]
    group_row = (shift_x & (CLASSES_X - 1)) * CLASSES_Y + shift_y
    group_col = column_of(group_row)
    high_col = column_of(shift_x) // CLASSES_X
    along0 = lax.broadcasted_iota(jnp.int32, (rows, rows), 0)
    along1 = lax.broadcasted_iota(jnp.int32, (rows, rows), 1)
    same = group_row == group_col
    each = rows // CLASSES
    rank_row = jnp.sum(jnp.where(same & (along0 < along1), 1.0, 0.0), axis=0, keepdims=True).astype(jnp.int32)
    rank_col = jnp.sum(jnp.where(same & (along1 < along0), 1.0, 0.0), axis=1, keepdims=True).astype(jnp.int32)
    pack = jnp.where(along0 == group_row * each + rank_row, 1.0, 0.0).astype(jnp.bfloat16)
    unpack = jnp.where(along1 == group_col * each + rank_col, 1.0, 0.0).astype(jnp.bfloat16)
    return group_col // CLASSES_Y, high_col, pack, unpack


def kernel(
    v_hbm, b_hbm, c1, c2, shear_in, shear_out, acc, or1, u_out, turn_out,
    v, vp, pk0, pk1, rv0, rv1, rp0, rp1, ok0, ok1, or0,
    lh, ll, rights, p_in, u_own, u_other, q_mix, turn_in,
    load_sem, pair_send, pair_recv, in_send, in_recv, out_send, out_recv,
):
    rows, columns = v.shape[1:]
    strips = columns // LANES
    piece = rows // CLASSES * strips
    lines = rows * strips
    kx, ky, af = lax.axis_index("kx"), lax.axis_index("ky"), lax.axis_index("af")
    x, y, z = kx & 3, ky & 3, (kx >> 2) * 4 + (ky >> 2)
    own = pl.multiple_of(af * rows, rows)
    other = pl.multiple_of((1 - af) * rows, rows)
    partner = (kx, ky, 1 - af)

    def place(step):
        tx, ty, tz = (x + (step >> 5)) & 3, (y + (step >> 3)) & 3, (z + step) & 7
        return (tz >> 2) * NX + tx, (tz & 3) * NY + ty

    loads = [pltpu.make_async_copy(v_hbm, v, load_sem.at[0]), pltpu.make_async_copy(b_hbm, acc, load_sem.at[1])]
    for load in loads:
        load.start()

    barrier = pltpu.get_barrier_semaphore()

    def greet(step, carry):
        tx, ty = place(step)
        pl.semaphore_signal(barrier, inc=1, device_id=(tx, ty, af), device_id_type=MESH)
        return carry

    lax.fori_loop(1, CLASSES, greet, 0)
    pl.semaphore_signal(barrier, inc=1, device_id=partner, device_id_type=MESH)

    class_col, high_col, pack, unpack = tables(shear_in, own, rows)
    p_in[...] = pack
    u_own[...] = unpack
    turn_in[...] = (high_col + (class_col + kx >= CLASSES_X).astype(jnp.int32)) & 1
    loads[0].wait()

    def pack_item(item, into):
        for tile in range(columns // 256):
            span = slice(tile * 256, tile * 256 + 256)
            field = jnp.where(turn_in[...] == 1, v[1 - item, :, span], v[item, :, span])
            high, low = halves(field)
            packed = product(p_in[...], high) + product(p_in[...], low)
            for half in range(2):
                into[pl.ds(2 * tile + half, rows, stride=strips), :] = packed[:, half * LANES : half * LANES + LANES]

    def send_item(source, target, send_sem, recv_sem):
        def send(step, carry):
            tx, ty = place(step)
            group = ((tx - kx) & (CLASSES_X - 1)) * CLASSES_Y + ((ty - ky) & (CLASSES_Y - 1))
            part = pl.ds(group * piece, piece)
            pltpu.make_async_remote_copy(
                src_ref=source.at[part],
                dst_ref=target.at[part],
                send_sem=send_sem,
                recv_sem=recv_sem,
                device_id=(tx, ty, af),
                device_id_type=MESH,
            ).start()
            return carry

        lax.fori_loop(1, CLASSES, send, 0)

    def wait_item(buffer, sem):
        part = buffer.at[pl.ds(piece, lines - piece)]
        pltpu.make_async_copy(part, part, sem).wait()

    def to_partner(source, target, place_of):
        return pltpu.make_async_remote_copy(
            src_ref=source,
            dst_ref=target,
            send_sem=pair_send.at[place_of],
            recv_sem=pair_recv.at[place_of],
            device_id=partner,
            device_id_type=MESH,
        )

    def plain(buffer):
        parts = [halves(buffer[pl.ds(strip, rows, stride=strips), :]) for strip in range(strips)]
        return jnp.concatenate([p[0] for p in parts], axis=1), jnp.concatenate([p[1] for p in parts], axis=1)

    def ladder(tile, rh, rl):
        span = slice(tile * 256, tile * 256 + 256)
        return product(lh[...], rh[:, span]) + product(ll[...], rh[:, span]) + product(lh[...], rl[:, span])

    pack_item(0, pk0)
    pl.semaphore_wait(barrier, CLASSES)

    send_item(pk0, rv0, in_send.at[0], in_recv.at[0])
    rv0[0:piece, :] = pk0[0:piece, :]
    pack_item(1, pk1)
    send_item(pk1, rv1, in_send.at[1], in_recv.at[1])
    rv1[0:piece, :] = pk1[0:piece, :]
    field_copy = to_partner(v, vp, 0)
    field_copy.start()

    u_other[...] = tables(shear_in, other, rows)[3]
    class_col, high_col, pack, unpack = tables(shear_out, own, rows)
    turn_out[...] = (high_col + (class_col > kx).astype(jnp.int32)) & 1
    u_out[...] = unpack
    q_mix[...] = product(pack, u_own[...]).astype(jnp.bfloat16)

    def crossed_item(item, arrived, arrived_pair, into):
        rh, rl = rights.at[0, 2 + item], rights.at[1, 2 + item]
        wait_item(arrived, in_recv.at[item])
        copy = to_partner(arrived, arrived_pair, 1 + item)
        copy.start()
        high, low = plain(arrived)
        rh[pl.ds(own, rows), :] = product(u_own[...], high).astype(jnp.bfloat16)
        rl[pl.ds(own, rows), :] = product(u_own[...], low).astype(jnp.bfloat16)
        left = product(q_mix[...], high) + product(q_mix[...], low)
        lh[...], ll[...] = halves(left * c2[item, 0])
        copy.wait()
        high, low = plain(arrived_pair)
        rh[pl.ds(other, rows), :] = product(u_other[...], high).astype(jnp.bfloat16)
        rl[pl.ds(other, rows), :] = product(u_other[...], low).astype(jnp.bfloat16)
        for tile in range(columns // 256):
            term = ladder(tile, rh, rl)
            for half in range(2):
                into[pl.ds(2 * tile + half, rows, stride=strips), :] = term[:, half * LANES : half * LANES + LANES]

    crossed_item(0, rv0, rp0, ok0)
    send_item(ok0, or0, out_send.at[0], out_recv.at[0])
    or0[0:piece, :] = ok0[0:piece, :]
    crossed_item(1, rv1, rp1, ok1)
    send_item(ok1, or1, out_send.at[1], out_recv.at[1])
    or1[0:piece, :] = ok1[0:piece, :]

    loads[1].wait()
    field_copy.wait()
    for item in range(2):
        rh, rl = rights.at[0, item], rights.at[1, item]
        rh[pl.ds(own, rows), :], rl[pl.ds(own, rows), :] = halves(v[item])
        rh[pl.ds(other, rows), :], rl[pl.ds(other, rows), :] = halves(vp[item])
        lh[...], ll[...] = halves(v[item] * c1[item, 0])
        for tile in range(columns // 256):
            span = slice(tile * 256, tile * 256 + 256)
            acc[item, :, span] = (1.0 - mixing) * v[item, :, span] + mixing * (acc[item, :, span] + ladder(tile, rh, rl))

    wait_item(or0, out_recv.at[0])
    high, low = plain(or0)
    term = mixing * (product(u_out[...], high) + product(u_out[...], low))
    turned = turn_out[...] == 1
    acc[0] += jnp.where(turned, 0.0, term)
    acc[1] += jnp.where(turned, term, 0.0)
    for item, (first, second) in enumerate(((pk0, ok0), (pk1, ok1))):
        wait_item(first, in_send.at[item])
        wait_item(second, out_send.at[item])
    wait_item(or1, out_recv.at[1])


def finish(acc, arrived, u_out, turn_out, out_hbm, out, store_sem):
    items, rows, columns = out.shape
    strips = columns // LANES
    turned = turn_out[...] == 1
    stores = []
    for tile in range(columns // 256):
        span = slice(tile * 256, tile * 256 + 256)
        parts = [halves(arrived[pl.ds(2 * tile + half, rows, stride=strips), :]) for half in range(2)]
        high, low = jnp.concatenate([p[0] for p in parts], axis=1), jnp.concatenate([p[1] for p in parts], axis=1)
        term = mixing * (product(u_out[...], high) + product(u_out[...], low))
        out[0, :, span] = acc[0, :, span] + jnp.where(turned, term, 0.0)
        out[1, :, span] = acc[1, :, span] + jnp.where(turned, 0.0, term)
        stores.append(pltpu.make_async_copy(out.at[:, :, span], out_hbm.at[:, :, span], store_sem.at[tile]))
        stores[-1].start()
    for store in stores:
        store.wait()


def body(vertex, bare_vertex, bubble_direct, bubble_crossed, shear_in, shear_out):
    items, _, _, rows, columns = vertex.shape
    shape = (items, rows, columns)
    lines = (rows * columns // LANES, LANES)
    vmem = pl.BlockSpec(memory_space=pltpu.VMEM)
    anywhere = pl.BlockSpec(memory_space=pl.ANY)
    wide, real = jnp.float32, jnp.bfloat16
    dma = pltpu.SemaphoreType.DMA
    partial, arrived, order, turn = pl.pallas_call(
        kernel,
        out_shape=[
            pltpu.VMEM(shape, wide),
            pltpu.VMEM(lines, wide),
            pltpu.VMEM((rows, rows), real),
            pltpu.VMEM((rows, 1), jnp.int32),
        ],
        in_specs=[anywhere, anywhere, vmem, vmem, vmem, vmem],
        out_specs=[vmem] * 4,
        scratch_shapes=[pltpu.VMEM(shape, wide)] * 2
        + [pltpu.VMEM(lines, wide)] * 9
        + [pltpu.VMEM((rows, columns), real)] * 2
        + [pltpu.VMEM((2, 4, columns, columns), real)]
        + [pltpu.VMEM((rows, rows), real)] * 4
        + [pltpu.VMEM((rows, 1), jnp.int32)]
        + [dma((2,)), dma((3,)), dma((3,)), dma((2,)), dma((2,)), dma((2,)), dma((2,))],
        compiler_params=pltpu.CompilerParams(
            collective_id=0, has_side_effects=True, vmem_limit_bytes=60 * 2**20
        ),
    )(
        vertex.reshape(shape),
        bare_vertex.reshape(shape),
        bubble_direct,
        bubble_crossed,
        shear_in,
        shear_out,
    )
    updated = pl.pallas_call(
        finish,
        out_shape=jax.ShapeDtypeStruct(shape, wide),
        in_specs=[vmem] * 4,
        out_specs=anywhere,
        scratch_shapes=[pltpu.VMEM(shape, wide), dma((columns // 256,))],
        compiler_params=pltpu.CompilerParams(vmem_limit_bytes=16 * 2**20),
    )(partial, arrived, order, turn)
    return updated.reshape(vertex.shape)


def solution(mesh):
    placed = (
        P(None, "kx", "ky", "af", None),
        P(None, "kx", "ky", "af", None),
        P(None, "kx", "ky", None),
        P(None, "kx", "ky", None),
        P(),
        P(),
    )
    return jax.shard_map(
        body, mesh=mesh, in_specs=placed, out_specs=P(None, "kx", "ky", "af", None), check_vma=False
    )
```

```python
import functools

import jax
import jax.numpy as jnp
from jax import lax
from jax.experimental import pallas as pl
from jax.experimental.pallas import tpu as pltpu
from jax.sharding import PartitionSpec as P

MESH = pl.DeviceIdType.MESH
mixing = 0.5
LANES = 128
NX, NY, NZ = 4, 4, 8
CLASSES_X, CLASSES_Y = 8, 16
CLASSES = CLASSES_X * CLASSES_Y


def halves(value):
    high = value.astype(jnp.bfloat16)
    low = (value - high.astype(jnp.float32)).astype(jnp.bfloat16)
    return high, low


def product(left, right):
    return jnp.dot(left, right, preferred_element_type=jnp.float32)


def column_of(row):
    wide = jnp.broadcast_to(row, (8, row.shape[1])).astype(jnp.float32)
    return wide.T[:, :1].astype(jnp.int32)


def tables(shear, first, rows):
    shift_x = shear[0:1, pl.ds(first, rows)]
    shift_y = shear[1:2, pl.ds(first, rows)]
    group_row = (shift_x & (CLASSES_X - 1)) * CLASSES_Y + shift_y
    group_col = column_of(group_row)
    high_col = column_of(shift_x) // CLASSES_X
    along0 = lax.broadcasted_iota(jnp.int32, (rows, rows), 0)
    along1 = lax.broadcasted_iota(jnp.int32, (rows, rows), 1)
    same = group_row == group_col
    each = rows // CLASSES
    rank_row = jnp.sum(jnp.where(same & (along0 < along1), 1.0, 0.0), axis=0, keepdims=True).astype(jnp.int32)
    rank_col = jnp.sum(jnp.where(same & (along1 < along0), 1.0, 0.0), axis=1, keepdims=True).astype(jnp.int32)
    pack = jnp.where(along0 == group_row * each + rank_row, 1.0, 0.0).astype(jnp.bfloat16)
    unpack = jnp.where(along1 == group_col * each + rank_col, 1.0, 0.0).astype(jnp.bfloat16)
    return group_col // CLASSES_Y, high_col, pack, unpack


def kernel(
    v_hbm, b_hbm, c1, c2, shear_in, shear_out, acc, or1, u_out, turn_out,
    v, vp, pk0, pk1, rv0, rv1, rp0, rp1, ok0, ok1, or0,
    lh, ll, rights, p_in, u_own, u_other, q_mix, turn_in,
    load_sem, pair_send, pair_recv, in_send, in_recv, out_send, out_recv,
):
    rows, columns = v.shape[1:]
    strips = columns // LANES
    piece = rows // CLASSES * strips
    lines = rows * strips
    kx, ky, af = lax.axis_index("kx"), lax.axis_index("ky"), lax.axis_index("af")
    x, y, z = kx & 3, ky & 3, (kx >> 2) * 4 + (ky >> 2)
    own = pl.multiple_of(af * rows, rows)
    other = pl.multiple_of((1 - af) * rows, rows)
    partner = (kx, ky, 1 - af)

    def place(step):
        tx, ty, tz = (x + (step >> 5)) & 3, (y + (step >> 3)) & 3, (z + step) & 7
        return (tz >> 2) * NX + tx, (tz & 3) * NY + ty

    def each_place(visit):
        def plane(at, carry):
            for step in range(NZ):
                visit(at * NZ + step, carry)
            return carry

        for step in range(1, NZ):
            visit(step, 0)
        lax.fori_loop(1, NX * NY, plane, 0)

    loads = [pltpu.make_async_copy(v_hbm, v, load_sem.at[0]), pltpu.make_async_copy(b_hbm, acc, load_sem.at[1])]
    for load in loads:
        load.start()

    barrier = pltpu.get_barrier_semaphore()

    def greet(step, carry):
        tx, ty = place(step)
        pl.semaphore_signal(barrier, inc=1, device_id=(tx, ty, af), device_id_type=MESH)
        return carry

    each_place(greet)
    pl.semaphore_signal(barrier, inc=1, device_id=partner, device_id_type=MESH)

    class_col, high_col, pack, unpack = tables(shear_in, own, rows)
    p_in[...] = pack
    u_own[...] = unpack
    turn_in[...] = (high_col + (class_col + kx >= CLASSES_X).astype(jnp.int32)) & 1
    loads[0].wait()

    def pack_item(item, into):
        for tile in range(columns // 256):
            span = slice(tile * 256, tile * 256 + 256)
            field = jnp.where(turn_in[...] == 1, v[1 - item, :, span], v[item, :, span])
            high, low = halves(field)
            packed = product(p_in[...], high) + product(p_in[...], low)
            for half in range(2):
                into[pl.ds(2 * tile + half, rows, stride=strips), :] = packed[:, half * LANES : half * LANES + LANES]

    def send_item(source, target, send_sem, recv_sem):
        def send(step, carry):
            tx, ty = place(step)
            group = ((tx - kx) & (CLASSES_X - 1)) * CLASSES_Y + ((ty - ky) & (CLASSES_Y - 1))
            part = pl.ds(group * piece, piece)
            pltpu.make_async_remote_copy(
                src_ref=source.at[part],
                dst_ref=target.at[part],
                send_sem=send_sem,
                recv_sem=recv_sem,
                device_id=(tx, ty, af),
                device_id_type=MESH,
            ).start()
            return carry

        each_place(send)

    def wait_item(buffer, sem):
        part = buffer.at[pl.ds(piece, lines - piece)]
        pltpu.make_async_copy(part, part, sem).wait()

    def to_partner(source, target, place_of):
        return pltpu.make_async_remote_copy(
            src_ref=source,
            dst_ref=target,
            send_sem=pair_send.at[place_of],
            recv_sem=pair_recv.at[place_of],
            device_id=partner,
            device_id_type=MESH,
        )

    def plain(buffer):
        parts = [halves(buffer[pl.ds(strip, rows, stride=strips), :]) for strip in range(strips)]
        return jnp.concatenate([p[0] for p in parts], axis=1), jnp.concatenate([p[1] for p in parts], axis=1)

    def ladder(tile, rh, rl):
        span = slice(tile * 256, tile * 256 + 256)
        return product(lh[...], rh[:, span]) + product(ll[...], rh[:, span]) + product(lh[...], rl[:, span])

    pack_item(0, pk0)
    pl.semaphore_wait(barrier, CLASSES)

    send_item(pk0, rv0, in_send.at[0], in_recv.at[0])
    rv0[0:piece, :] = pk0[0:piece, :]
    pack_item(1, pk1)
    send_item(pk1, rv1, in_send.at[1], in_recv.at[1])
    rv1[0:piece, :] = pk1[0:piece, :]
    field_copy = to_partner(v, vp, 0)
    field_copy.start()

    u_other[...] = tables(shear_in, other, rows)[3]
    class_col, high_col, pack, unpack = tables(shear_out, own, rows)
    turn_out[...] = (high_col + (class_col > kx).astype(jnp.int32)) & 1
    u_out[...] = unpack
    q_mix[...] = product(pack, u_own[...]).astype(jnp.bfloat16)

    def crossed_item(item, arrived, arrived_pair, into):
        rh, rl = rights.at[0, 2 + item], rights.at[1, 2 + item]
        wait_item(arrived, in_recv.at[item])
        copy = to_partner(arrived, arrived_pair, 1 + item)
        copy.start()
        high, low = plain(arrived)
        rh[pl.ds(own, rows), :] = product(u_own[...], high).astype(jnp.bfloat16)
        rl[pl.ds(own, rows), :] = product(u_own[...], low).astype(jnp.bfloat16)
        left = product(q_mix[...], high) + product(q_mix[...], low)
        lh[...], ll[...] = halves(left * c2[item, 0])
        copy.wait()
        high, low = plain(arrived_pair)
        rh[pl.ds(other, rows), :] = product(u_other[...], high).astype(jnp.bfloat16)
        rl[pl.ds(other, rows), :] = product(u_other[...], low).astype(jnp.bfloat16)
        for tile in range(columns // 256):
            term = ladder(tile, rh, rl)
            for half in range(2):
                into[pl.ds(2 * tile + half, rows, stride=strips), :] = term[:, half * LANES : half * LANES + LANES]

    crossed_item(0, rv0, rp0, ok0)
    send_item(ok0, or0, out_send.at[0], out_recv.at[0])
    or0[0:piece, :] = ok0[0:piece, :]
    crossed_item(1, rv1, rp1, ok1)
    send_item(ok1, or1, out_send.at[1], out_recv.at[1])
    or1[0:piece, :] = ok1[0:piece, :]

    loads[1].wait()
    field_copy.wait()
    for item in range(2):
        rh, rl = rights.at[0, item], rights.at[1, item]
        rh[pl.ds(own, rows), :], rl[pl.ds(own, rows), :] = halves(v[item])
        rh[pl.ds(other, rows), :], rl[pl.ds(other, rows), :] = halves(vp[item])
        lh[...], ll[...] = halves(v[item] * c1[item, 0])
        for tile in range(columns // 256):
            span = slice(tile * 256, tile * 256 + 256)
            acc[item, :, span] = (1.0 - mixing) * v[item, :, span] + mixing * (acc[item, :, span] + ladder(tile, rh, rl))

    wait_item(or0, out_recv.at[0])
    high, low = plain(or0)
    term = mixing * (product(u_out[...], high) + product(u_out[...], low))
    turned = turn_out[...] == 1
    acc[0] += jnp.where(turned, 0.0, term)
    acc[1] += jnp.where(turned, term, 0.0)
    for item, (first, second) in enumerate(((pk0, ok0), (pk1, ok1))):
        wait_item(first, in_send.at[item])
        wait_item(second, out_send.at[item])
    wait_item(or1, out_recv.at[1])


def finish(acc, arrived, u_out, turn_out, out_hbm, out, store_sem):
    items, rows, columns = out.shape
    strips = columns // LANES
    turned = turn_out[...] == 1
    stores = []
    for tile in range(columns // 256):
        span = slice(tile * 256, tile * 256 + 256)
        parts = [halves(arrived[pl.ds(2 * tile + half, rows, stride=strips), :]) for half in range(2)]
        high, low = jnp.concatenate([p[0] for p in parts], axis=1), jnp.concatenate([p[1] for p in parts], axis=1)
        term = mixing * (product(u_out[...], high) + product(u_out[...], low))
        out[0, :, span] = acc[0, :, span] + jnp.where(turned, term, 0.0)
        out[1, :, span] = acc[1, :, span] + jnp.where(turned, 0.0, term)
        stores.append(pltpu.make_async_copy(out.at[:, :, span], out_hbm.at[:, :, span], store_sem.at[tile]))
        stores[-1].start()
    for store in stores:
        store.wait()


def body(vertex, bare_vertex, bubble_direct, bubble_crossed, shear_in, shear_out):
    items, _, _, rows, columns = vertex.shape
    shape = (items, rows, columns)
    lines = (rows * columns // LANES, LANES)
    vmem = pl.BlockSpec(memory_space=pltpu.VMEM)
    anywhere = pl.BlockSpec(memory_space=pl.ANY)
    wide, real = jnp.float32, jnp.bfloat16
    dma = pltpu.SemaphoreType.DMA
    partial, arrived, order, turn = pl.pallas_call(
        kernel,
        out_shape=[
            pltpu.VMEM(shape, wide),
            pltpu.VMEM(lines, wide),
            pltpu.VMEM((rows, rows), real),
            pltpu.VMEM((rows, 1), jnp.int32),
        ],
        in_specs=[anywhere, anywhere, vmem, vmem, vmem, vmem],
        out_specs=[vmem] * 4,
        scratch_shapes=[pltpu.VMEM(shape, wide)] * 2
        + [pltpu.VMEM(lines, wide)] * 9
        + [pltpu.VMEM((rows, columns), real)] * 2
        + [pltpu.VMEM((2, 4, columns, columns), real)]
        + [pltpu.VMEM((rows, rows), real)] * 4
        + [pltpu.VMEM((rows, 1), jnp.int32)]
        + [dma((2,)), dma((3,)), dma((3,)), dma((2,)), dma((2,)), dma((2,)), dma((2,))],
        compiler_params=pltpu.CompilerParams(
            collective_id=0, has_side_effects=True, vmem_limit_bytes=60 * 2**20
        ),
    )(
        vertex.reshape(shape),
        bare_vertex.reshape(shape),
        bubble_direct,
        bubble_crossed,
        shear_in,
        shear_out,
    )
    updated = pl.pallas_call(
        finish,
        out_shape=jax.ShapeDtypeStruct(shape, wide),
        in_specs=[vmem] * 4,
        out_specs=anywhere,
        scratch_shapes=[pltpu.VMEM(shape, wide), dma((columns // 256,))],
        compiler_params=pltpu.CompilerParams(vmem_limit_bytes=16 * 2**20),
    )(partial, arrived, order, turn)
    return updated.reshape(vertex.shape)


def solution(mesh):
    placed = (
        P(None, "kx", "ky", "af", None),
        P(None, "kx", "ky", "af", None),
        P(None, "kx", "ky", None),
        P(None, "kx", "ky", None),
        P(),
        P(),
    )
    return jax.shard_map(
        body, mesh=mesh, in_specs=placed, out_specs=P(None, "kx", "ky", "af", None), check_vma=False
    )
```
